512 devices in a mesh: rep: 16 (over z_hi, y), dp: 32 (over x, z_lo, core).
Axes of the slice: x: 4, y: 8, z: 8 (z_hi: 2, z_lo: 4; z = z_hi * 4 + z_lo), core: 2. Of those that a mesh axis runs over, the one named last changes fastest.
Arguments:
- old_master: float32 [16, 512, 128], P('rep'), may hold values from -0.6 to 0.6
- old_first: float32 [16, 512, 128], P('rep'), may hold values from -6 to 6
- old_second: float32 [16, 512, 128], P('rep'), may hold values from 0.1 to 4
- grad_parts: bfloat16 [16, 32, 4096, 128], P('rep', 'dp'), may hold values from -0.3984375 to 0.3984375
- section_rows: int32 [16], replicated, may hold values from 1 to 512, 4096 in all
- adam_step: int32 [1], replicated, may hold values from 1 to 63
Outputs:
- new_master: float32 [4096, 128], P('dp')
- new_first: float32 [4096, 128], P('dp')
- new_second: float32 [4096, 128], P('dp')
- direction: float32 [4096, 128], P('dp')
The draws below stay inside these ranges and needn't reach their ends.
Inputs may be any that keep to these rules, and one draw needn't show every extreme that they name: `section_rows`: lengths of the sections, summing to 4096; some section has exactly 512 rows.
All inputs are finite; a program needn't handle non-finite values.
Results may differ from the reference program's by a relative error of at most 0.0003.
Values sent between devices are 32-bit elements; how exact they have to be, the bound alone decides.
No kernel may reach another device: no remote copies, remote signals or barrier semaphores. Data moves between devices by JAX's collectives and lax.ppermute only.
A program may use at most 64 MiB of HBM per device.

```python
import math
import jax
import jax.numpy as jnp
import numpy as np
from jax import lax

LANES = 128
ROWS = 4096
CAP = 512
N_REP = 16
N_DP = 32


def strengthened(values, own_key, source, target, blocks, factor):
    owner, partner = [(jnp.arange(values.shape[axis_at]) // (values.shape[axis_at] // blocks)).reshape([-1 if axis == axis_at else 1 for axis in range(values.ndim)]) for axis_at in (source, target)]
    chosen = jax.random.permutation(own_key, blocks)[partner]
    strong = (owner == chosen) | (owner == (partner + blocks // 2) % blocks)
    return jnp.where(strong, factor * values, values)


def levels(stream_key, extent, cuts, smallest, top_value):
    gain = 1.0
    for position, shards_of in cuts:
        heights = jax.random.uniform(jax.random.fold_in(jax.random.fold_in(stream_key, 6), position), (shards_of,), jnp.float32, smallest / len(cuts), top_value / len(cuts))
        gain = gain * jnp.repeat(jnp.exp(heights), extent[position] // shards_of).reshape((-1,) + (1,) * (len(extent) - 1 - position))
    return gain


def split_up(amount, total, bound, skew):
    loads = [(1 << 20) // math.isqrt(grade ** skew) + 1 for grade in range(2, amount + 1)]
    surplus, given = total - bound - (amount - 1), [1] * (amount - 1)
    while surplus > 0:
        movable = [i for i in range(amount - 1) if given[i] < bound]
        mass, remaining = sum([loads[i] for i in movable]), surplus
        for i in movable:
            addition = min(bound - given[i], max(1, remaining * loads[i] // mass), surplus)
            given[i] = given[i] + addition
            surplus = surplus - addition
    return np.array([bound] + given)


def uneven_parts(stream_key, amount, total, reach, lean):
    if amount == 2:
        one = jax.random.randint(stream_key, (), max(1, total - reach), min(reach, total - 1) + 1)
        return jnp.stack([one, total - one])
    lengths = jnp.asarray(split_up(amount, total, reach, lean), jnp.int32)
    twos = (amount - 1) // 2
    source_of, receiver = lengths[1:1 + 2 * twos:2], lengths[2:2 + 2 * twos:2]
    room = jnp.minimum(source_of - 1, reach - receiver)
    passed = jax.random.randint(jax.random.fold_in(stream_key, 1), (twos,), 0, 1 << 20) % (room + 1)
    lengths = lengths.at[1:1 + 2 * twos:2].set(source_of - passed).at[2:2 + 2 * twos:2].set(receiver + passed)
    return lengths[jax.random.permutation(jax.random.fold_in(stream_key, 2), amount)]


def normal_values(key, extent, scale, bound, split=(), held_as=jnp.bfloat16):
    entries = jax.random.normal(key, extent, jnp.float32) * scale
    if len(split) > 0:
        entries = levels(key, extent, split, -0.22, 0.18) * entries
    return jnp.clip(entries, min=-bound, max=bound).astype(held_as)


def heavy_noise(stream_key, shape, width, most, split, heavy, kind=jnp.bfloat16):
    values = width * jax.random.normal(stream_key, shape, jnp.float32)
    if split:
        values = values * levels(stream_key, shape, split, -0.22, 0.18)
    return jnp.clip(strengthened(values, jax.random.fold_in(stream_key, 3), *heavy), -most, most).astype(kind)


def setup_inputs(seed: int = 0) -> dict:
    key_list = jax.random.split(jax.random.key(seed), 7)
    return {
        "old_master": normal_values(key_list[0], (N_REP, CAP, LANES), 0.1, 0.6, ((0, 16),), jnp.float32),
        "old_first": normal_values(key_list[1], (N_REP, CAP, LANES), 1.0, 6.0, ((0, 16),), jnp.float32),
        "old_second": jnp.clip(jnp.exp(math.log(4.0) - 3.6888794 * jax.random.uniform(key_list[2], (N_REP, CAP, LANES), jnp.float32) ** levels(key_list[2], (N_REP, CAP, LANES), ((0, 16),), -0.2, 0.2)), 0.1, 4.0),
        "grad_parts": heavy_noise(key_list[3], (N_REP, N_DP, ROWS, LANES), 0.05, 0.3984375, ((0, 16), (1, 32)), (1, 2, 32, 2.75)),
        "section_rows": uneven_parts(key_list[4], N_REP, ROWS, CAP, 2).astype(jnp.int32),
        "adam_step": jax.random.randint(key_list[5], (1,), 1, 64).astype(jnp.int32),
    }


BETA_ONE = 0.9
BETA_TWO = 0.999
EPSILON = 1e-08
RATE = 0.01
DECAY = 0.1

def relay(old_state, section_rows):
    section_ends = jnp.cumsum(section_rows).astype(jnp.int32)
    section_begins = (section_ends - section_rows).astype(jnp.int32)
    flat_rows = jnp.arange(ROWS, dtype=jnp.int32)
    owners = lax.optimization_barrier(jnp.sum((flat_rows[:, None] >= section_ends[None, :]).astype(jnp.int32), axis=1)).astype(jnp.int32)
    local_row = (flat_rows - section_begins[owners]).astype(jnp.int32)
    return old_state[owners, local_row]

def adam_update(master, first, second, gradient, adam_step):
    counted = adam_step[0].astype(jnp.float32)
    new_first = BETA_ONE * first + (1.0 - BETA_ONE) * gradient
    new_second = BETA_TWO * second + (1.0 - BETA_TWO) * gradient * gradient
    first_fix = 1.0 - jnp.power(jnp.float32(BETA_ONE), counted)
    second_fix = 1.0 - jnp.power(jnp.float32(BETA_TWO), counted)
    direction = new_first / first_fix / (jnp.sqrt(new_second / second_fix) + EPSILON)
    new_master = master - RATE * (direction + DECAY * master)
    return (new_master, new_first, new_second, direction)

def reference(old_master, old_first, old_second, grad_parts, section_rows, adam_step):
    master = relay(old_master, section_rows)
    first = relay(old_first, section_rows)
    second = relay(old_second, section_rows)

    def add_replica(total, replica):
        return (total + lax.optimization_barrier(jnp.sum(replica.astype(jnp.float32), axis=0)), None)
    gradient, _ = lax.scan(add_replica, jnp.zeros((ROWS, LANES), jnp.float32), grad_parts)
    new_master, new_first, new_second, direction = adam_update(master, first, second, gradient, adam_step)
    return (new_master, new_first, new_second, direction)
```

```python
import jax
import jax.numpy as jnp
from jax import lax
from jax.sharding import PartitionSpec as P

BETA_ONE = 0.9
BETA_TWO = 0.999
EPSILON = 1e-08
RATE = 0.01
DECAY = 0.1
LANES = 128
BITS = (0, 1)


def dp_index(x, z_two, z_one, core):
    return x * 8 + z_two * 4 + z_one * 2 + core


def rep_index(z_hi, y_high, y_one):
    return z_hi * 8 + y_high * 2 + y_one


def flat_index(x, z_two, z_one, core, z_hi, y_high, y_one):
    return rep_index(z_hi, y_high, y_one) * 32 + dp_index(x, z_two, z_one, core)


SPREAD_GROUPS = [
    [flat_index(x, z_two, z_one, core, z_hi, y_high, y_one) for x in range(4) for z_one in BITS for y_one in BITS]
    for z_hi in BITS for y_high in range(4) for z_two in BITS for core in BITS
]
FAR_GROUPS = [
    [flat_index(x, z_two, z_one, core, z_hi, y_high, y_one) for z_two in BITS for z_hi in BITS for y_high in range(4)]
    for y_one in BITS for x in range(4) for z_one in BITS for core in BITS
]
GATHER_GROUPS = [
    [rep_index(z_hi, y_high, y_one) for y_one in BITS for y_high in range(4)] for z_hi in BITS
]
CORE_PAIRS = [(d, d ^ 1) for d in range(32)]
Y_PAIRS = [(r, r ^ 1) for r in range(16)]


def adam_update(master, first, second, gradient, adam_step):
    counted = adam_step[0].astype(jnp.float32)
    new_first = BETA_ONE * first + (1.0 - BETA_ONE) * gradient
    new_second = BETA_TWO * second + (1.0 - BETA_TWO) * gradient * gradient
    first_fix = 1.0 - jnp.power(jnp.float32(BETA_ONE), counted)
    second_fix = 1.0 - jnp.power(jnp.float32(BETA_TWO), counted)
    direction = new_first / first_fix / (jnp.sqrt(new_second / second_fix) + EPSILON)
    new_master = master - RATE * (direction + DECAY * master)
    return (new_master, new_first, new_second, direction)


def state_rows(sections, section_rows, rank_rep, first_shard, z_two):
    owners = jnp.arange(section_rows.shape[0], dtype=jnp.int32)
    begin = jnp.sum(jnp.where(owners < rank_rep, section_rows, 0))
    length = jnp.sum(jnp.where(owners == rank_rep, section_rows, 0))
    capacity = sections[0].shape[1]
    padded = [jnp.pad(section[0], ((128, 128), (0, 0))) for section in sections]
    chosen = []
    for other in BITS:
        first_row = (first_shard + other * 4) * 128 - begin
        start = jnp.clip(first_row + 128, 0, capacity + 128)
        positions = first_row + jnp.arange(128, dtype=jnp.int32)
        usable = ((positions >= 0) & (positions < length))[:, None]
        for section in padded:
            window = lax.dynamic_slice_in_dim(section, start, 128, 0)
            window = jnp.where(usable, window, 0.0).reshape(2, 4, 2, 8, LANES)
            chosen.append(lax.dynamic_index_in_dim(window, z_two, 2, keepdims=False))
    return jnp.stack(chosen).reshape(2, 3, 2, 4, 8, LANES)


def local(old_master, old_first, old_second, grad_parts, section_rows, adam_step):
    rank_rep = lax.axis_index("rep")
    rank_dp = lax.axis_index("dp")
    core = rank_dp % 2
    z_two = (rank_dp // 4) % 2
    y_one = rank_rep % 2
    parts = grad_parts.reshape(4, 2, 2, 2, 2, 64, LANES)
    parts = jnp.transpose(parts, (3, 0, 2, 4, 1, 5, 6))
    given = lax.dynamic_index_in_dim(parts, 1 - core, 0, keepdims=False).astype(jnp.float32)
    kept = lax.dynamic_index_in_dim(parts, core, 0, keepdims=False).astype(jnp.float32)
    taken = lax.ppermute(given, "dp", CORE_PAIRS)
    rows = state_rows((old_master, old_first, old_second), section_rows, rank_rep, rank_dp - z_two * 4, z_two)
    other_rows = lax.dynamic_index_in_dim(rows, 1 - y_one, 2, keepdims=False)
    own_rows = lax.dynamic_index_in_dim(rows, y_one, 2, keepdims=False)
    pair_rows = own_rows + lax.ppermute(other_rows, "rep", Y_PAIRS)
    spread = (kept + taken).reshape(16, 128, LANES)
    spread = lax.all_to_all(spread, ("rep", "dp"), 0, 0, axis_index_groups=SPREAD_GROUPS)
    near_sum = jnp.sum(spread, axis=0).reshape(2, 1, 4, 16, LANES)
    near_sum = jnp.broadcast_to(near_sum, (2, 2, 4, 16, LANES))
    state = jnp.transpose(pair_rows, (0, 2, 1, 3, 4)).reshape(2, 1, 4, 24, LANES)
    state = jnp.broadcast_to(state, (2, 2, 4, 24, LANES))
    far = jnp.concatenate([near_sum, state], axis=3).reshape(16, 40, LANES)
    far = lax.all_to_all(far, ("rep", "dp"), 0, 0, axis_index_groups=FAR_GROUPS)
    gradient = jnp.sum(far[:, :16], axis=0)
    state = jnp.sum(far[:, 16:].reshape(2, 8, 3, 8, LANES), axis=1)
    state = jnp.transpose(state, (1, 0, 2, 3)).reshape(3, 16, LANES)
    new = jnp.stack(adam_update(state[0], state[1], state[2], gradient, adam_step))
    new = jnp.broadcast_to(new[None], (8, 4, 16, LANES))
    new = lax.all_to_all(new, "rep", 0, 0, axis_index_groups=GATHER_GROUPS)
    return tuple(new[:, i].reshape(128, LANES) for i in range(4))


def solution(mesh):
    in_specs = (
        P("rep", None, None),
        P("rep", None, None),
        P("rep", None, None),
        P("rep", "dp", None, None),
        P(),
        P(),
    )
    out_specs = (P("dp", None), P("dp", None), P("dp", None), P("dp", None))
    return jax.shard_map(local, mesh=mesh, in_specs=in_specs, out_specs=out_specs, check_vma=False)
```

```python
import jax
import jax.numpy as jnp
from jax import lax
from jax.experimental import pallas as pl
from jax.experimental.pallas import tpu as pltpu
from jax.sharding import PartitionSpec as P

BETA_ONE = 0.9
BETA_TWO = 0.999
EPSILON = 1e-08
RATE = 0.01
DECAY = 0.1
LANES = 128
CAP = 512
SHARD = 128
PIECE = 16
EIGHT = 8
BITS = (0, 1)
VMEM = pl.BlockSpec(memory_space=pltpu.VMEM)


def dp_index(x, z_two, z_one, core):
    return x * 8 + z_two * 4 + z_one * 2 + core


def rep_index(z_hi, y_high, y_one):
    return z_hi * 8 + y_high * 2 + y_one


def flat_index(x, z_two, z_one, core, z_hi, y_high, y_one):
    return rep_index(z_hi, y_high, y_one) * 32 + dp_index(x, z_two, z_one, core)


SPREAD_GROUPS = [
    [flat_index(x, z_two, z_one, core, z_hi, y_high, y_one) for x in range(4) for z_one in BITS for y_one in BITS]
    for z_hi in BITS for y_high in range(4) for z_two in BITS for core in BITS
]
FAR_GROUPS = [
    [flat_index(x, z_two, z_one, core, z_hi, y_high, y_one) for z_two in BITS for z_hi in BITS for y_high in range(4)]
    for y_one in BITS for x in range(4) for z_one in BITS for core in BITS
]
GATHER_GROUPS = [
    [rep_index(z_hi, y_high, y_one) for y_one in BITS for y_high in range(4)] for z_hi in BITS
]
CORE_PAIRS = [(d, d ^ 1) for d in range(32)]


def adam_update(master, first, second, gradient, adam_step):
    counted = adam_step[0].astype(jnp.float32)
    new_first = BETA_ONE * first + (1.0 - BETA_ONE) * gradient
    new_second = BETA_TWO * second + (1.0 - BETA_TWO) * gradient * gradient
    first_fix = 1.0 - jnp.power(jnp.float32(BETA_ONE), counted)
    second_fix = 1.0 - jnp.power(jnp.float32(BETA_TWO), counted)
    direction = new_first / first_fix / (jnp.sqrt(new_second / second_fix) + EPSILON)
    new_master = master - RATE * (direction + DECAY * master)
    return (new_master, new_first, new_second, direction)


def state_kernel(rows_ref, master_ref, first_ref, second_ref, out_ref, held, sems):
    copies = [
        pltpu.make_async_copy(source.at[0], held.at[i, pl.ds(EIGHT, CAP)], sems.at[i])
        for i, source in enumerate((master_ref, first_ref, second_ref))
    ]
    for copy in copies:
        copy.start()
    rank_rep = lax.axis_index("rep")
    rank_dp = lax.axis_index("dp")
    core = rank_dp % 2
    z_one = (rank_dp // 2) % 2
    z_two = (rank_dp // 4) % 2
    turn = (rank_dp // 8) * 2 + z_one
    begin = jnp.int32(0)
    length = jnp.int32(0)
    for owner in range(16):
        held_rows = rows_ref[owner]
        begin += jnp.where(owner < rank_rep, held_rows, 0)
        length += jnp.where(owner == rank_rep, held_rows, 0)
    base = (turn // 4) * (4 * SHARD) + core * SHARD + (turn % 4) * PIECE + z_two * EIGHT - begin
    place = lax.broadcasted_iota(jnp.int32, (EIGHT, LANES), 0)
    for copy in copies:
        copy.wait()
    for peer in range(16):
        x, other_z, other_y = peer // 4, (peer // 2) % 2, peer % 2
        start = base + x * (8 * SHARD) + other_z * (2 * SHARD) + other_y * (SHARD // 2)
        usable = (place >= -start) & (place < length - start)
        at = jnp.clip(start, -EIGHT, CAP) + EIGHT
        for i in range(3):
            rows = held[i, pl.ds(at, EIGHT), :]
            out_ref[peer, i * EIGHT : (i + 1) * EIGHT, :] = jnp.where(usable, rows, 0.0)


def add_kernel(taken_ref, grad_ref, state_ref, out_ref):
    core = lax.axis_index("dp") % 2
    half = SHARD // 2
    for x in range(4):
        for z_two in BITS:
            for z_one in BITS:
                block = x * 4 + z_two * 2 + z_one
                own = pl.multiple_of((block * 2 + core) * SHARD, SHARD)
                total = taken_ref[pl.ds(block * SHARD, SHARD), :] + grad_ref[pl.ds(own, SHARD), :].astype(jnp.float32)
                for y_one in BITS:
                    peer = x * 4 + z_one * 2 + y_one
                    out_ref[peer, z_two * half : (z_two + 1) * half, :] = total[y_one * half : (y_one + 1) * half]
    out_ref[:, SHARD:, :] = state_ref[...]


def near_kernel(in_ref, out_ref):
    for z_two in BITS:
        for y_high in range(4):
            turn = z_two * 4 + y_high
            rows = pl.ds(turn * PIECE, PIECE)
            total = in_ref[0, rows, :]
            for peer in range(1, 16):
                total += in_ref[peer, rows, :]
            state = in_ref[2 * turn, SHARD:, :] + in_ref[2 * turn + 1, SHARD:, :]
            for z_hi in BITS:
                slot = z_two * 8 + z_hi * 4 + y_high
                out_ref[slot, :PIECE, :] = total
                out_ref[slot, PIECE:, :] = state


def local(old_master, old_first, old_second, grad_parts, section_rows, adam_step):
    core = lax.axis_index("dp") % 2
    grads = grad_parts.reshape(32 * SHARD, LANES)
    given = lax.dynamic_index_in_dim(grad_parts.reshape(16, 2, SHARD, LANES), 1 - core, 1, keepdims=False)
    taken = lax.ppermute(given.astype(jnp.float32).reshape(16 * SHARD, LANES), "dp", CORE_PAIRS)
    any_space = pl.BlockSpec(memory_space=pl.ANY)
    state = pl.pallas_call(
        state_kernel,
        out_shape=jax.ShapeDtypeStruct((16, 24, LANES), jnp.float32),
        in_specs=[pl.BlockSpec(memory_space=pltpu.SMEM), any_space, any_space, any_space],
        out_specs=VMEM,
        scratch_shapes=[pltpu.VMEM((3, CAP + 2 * EIGHT, LANES), jnp.float32), pltpu.SemaphoreType.DMA((3,))],
        cost_estimate=pl.CostEstimate(flops=100_000, bytes_accessed=1_000_000, transcendentals=0),
    )(section_rows, old_master, old_first, old_second)
    spread = pl.pallas_call(
        add_kernel,
        out_shape=jax.ShapeDtypeStruct((16, 152, LANES), jnp.float32),
        in_specs=[VMEM, VMEM, VMEM],
        out_specs=VMEM,
        compiler_params=pltpu.CompilerParams(vmem_limit_bytes=32 * 1024 * 1024),
    )(taken, grads, state)
    spread = lax.all_to_all(spread, ("rep", "dp"), 0, 0, axis_index_groups=SPREAD_GROUPS)
    far = pl.pallas_call(
        near_kernel,
        out_shape=jax.ShapeDtypeStruct((16, 40, LANES), jnp.float32),
        in_specs=[VMEM],
        out_specs=VMEM,
    )(spread)
    far = lax.all_to_all(far, ("rep", "dp"), 0, 0, axis_index_groups=FAR_GROUPS)
    gradient = jnp.sum(far[:, :PIECE], axis=0)
    state = jnp.sum(far[:, PIECE:].reshape(2, 8, 3, EIGHT, LANES), axis=1)
    state = jnp.transpose(state, (1, 0, 2, 3)).reshape(3, PIECE, LANES)
    new = jnp.stack(adam_update(state[0], state[1], state[2], gradient, adam_step))
    new = jnp.broadcast_to(new[None], (8, 4, PIECE, LANES))
    new = lax.all_to_all(new, "rep", 0, 0, axis_index_groups=GATHER_GROUPS)
    return tuple(new[:, i].reshape(SHARD, LANES) for i in range(4))


def solution(mesh):
    in_specs = (
        P("rep", None, None),
        P("rep", None, None),
        P("rep", None, None),
        P("rep", "dp", None, None),
        P(),
        P(),
    )
    out_specs = (P("dp", None), P("dp", None), P("dp", None), P("dp", None))
    return jax.shard_map(local, mesh=mesh, in_specs=in_specs, out_specs=out_specs, check_vma=False)
```

```python
import jax
import jax.numpy as jnp
from jax import lax
from jax.experimental import pallas as pl
from jax.experimental.pallas import tpu as pltpu
from jax.sharding import PartitionSpec as P

BETA_ONE = 0.9
BETA_TWO = 0.999
EPSILON = 1e-08
RATE = 0.01
DECAY = 0.1
LANES = 128
CAP = 512
SHARD = 128
PIECE = 16
EIGHT = 8
BITS = (0, 1)
VMEM = pl.BlockSpec(memory_space=pltpu.VMEM)
SMALL = pltpu.CompilerParams(vmem_limit_bytes=8 * 1024 * 1024)


def dp_index(x, z_two, z_one, core):
    return x * 8 + z_two * 4 + z_one * 2 + core


def rep_index(z_hi, y_high, y_one):
    return z_hi * 8 + y_high * 2 + y_one


def flat_index(x, z_two, z_one, core, z_hi, y_high, y_one):
    return rep_index(z_hi, y_high, y_one) * 32 + dp_index(x, z_two, z_one, core)


SPREAD_GROUPS = [
    [flat_index(x, z_two, z_one, core, z_hi, y_high, y_one) for x in range(4) for z_one in BITS for y_one in BITS]
    for z_hi in BITS for y_high in range(4) for z_two in BITS for core in BITS
]
FAR_GROUPS = [
    [flat_index(x, z_two, z_one, core, z_hi, y_high, y_one) for z_two in BITS for z_hi in BITS for y_high in range(4)]
    for y_one in BITS for x in range(4) for z_one in BITS for core in BITS
]
GATHER_GROUPS = [
    [rep_index(z_hi, y_high, y_one) for y_one in BITS for y_high in range(4)] for z_hi in BITS
]
CORE_PAIRS = [(d, d ^ 1) for d in range(32)]


def corrections(adam_step):
    counted = adam_step[0].astype(jnp.float32)
    first_fix = 1.0 - jnp.power(jnp.float32(BETA_ONE), counted)
    second_fix = 1.0 - jnp.power(jnp.float32(BETA_TWO), counted)
    return first_fix, second_fix


def direction_of(new_first, new_second, first_fix, second_fix):
    return new_first / first_fix / (jnp.sqrt(new_second / second_fix) + EPSILON)


def state_kernel(rows_ref, master_ref, first_ref, second_ref, out_ref, held, sems):
    copies = [
        pltpu.make_async_copy(source.at[0], held.at[i, pl.ds(EIGHT, CAP)], sems.at[i])
        for i, source in enumerate((master_ref, first_ref, second_ref))
    ]
    for copy in copies:
        copy.start()
    rank_rep = lax.axis_index("rep")
    rank_dp = lax.axis_index("dp")
    core = rank_dp % 2
    z_one = (rank_dp // 2) % 2
    z_two = (rank_dp // 4) % 2
    turn = (rank_dp // 8) * 2 + z_one
    begin = jnp.int32(0)
    length = jnp.int32(0)
    for owner in range(16):
        held_rows = rows_ref[owner]
        begin += jnp.where(owner < rank_rep, held_rows, 0)
        length += jnp.where(owner == rank_rep, held_rows, 0)
    base = (turn // 4) * (4 * SHARD) + core * SHARD + (turn % 4) * PIECE + z_two * EIGHT - begin
    place = lax.broadcasted_iota(jnp.int32, (EIGHT, LANES), 0)
    for copy in copies:
        copy.wait()
    for peer in range(16):
        x, other_z, other_y = peer // 4, (peer // 2) % 2, peer % 2
        start = base + x * (8 * SHARD) + other_z * (2 * SHARD) + other_y * (SHARD // 2)
        usable = (place >= -start) & (place < length - start)
        at = jnp.clip(start, -EIGHT, CAP) + EIGHT
        for i in range(3):
            rows = held[i, pl.ds(at, EIGHT), :]
            out_ref[peer, i * EIGHT : (i + 1) * EIGHT, :] = jnp.where(usable, rows, 0.0)


def add_kernel(taken_ref, grad_ref, state_ref, out_ref):
    core = lax.axis_index("dp") % 2
    half = SHARD // 2
    for x in range(4):
        for z_two in BITS:
            for z_one in BITS:
                block = x * 4 + z_two * 2 + z_one
                own = pl.multiple_of((block * 2 + core) * SHARD, SHARD)
                total = taken_ref[pl.ds(block * SHARD, SHARD), :] + grad_ref[pl.ds(own, SHARD), :].astype(jnp.float32)
                for y_one in BITS:
                    peer = x * 4 + z_one * 2 + y_one
                    out_ref[peer, z_two * half : (z_two + 1) * half, :] = total[y_one * half : (y_one + 1) * half]
    out_ref[:, SHARD:, :] = state_ref[...]


def near_kernel(in_ref, out_ref):
    for z_two in BITS:
        for y_high in range(4):
            turn = z_two * 4 + y_high
            rows = pl.ds(turn * PIECE, PIECE)
            total = in_ref[0, rows, :]
            for peer in range(1, 16):
                total += in_ref[peer, rows, :]
            state = in_ref[2 * turn, SHARD:, :] + in_ref[2 * turn + 1, SHARD:, :]
            for z_hi in BITS:
                slot = z_two * 8 + z_hi * 4 + y_high
                out_ref[slot, :PIECE, :] = total
                out_ref[slot, PIECE:, :] = state


def local(old_master, old_first, old_second, grad_parts, section_rows, adam_step):
    core = lax.axis_index("dp") % 2
    grads = grad_parts.reshape(32 * SHARD, LANES)
    given = lax.dynamic_index_in_dim(grad_parts.reshape(16, 2, SHARD, LANES), 1 - core, 1, keepdims=False)
    taken = lax.ppermute(given.astype(jnp.float32).reshape(16 * SHARD, LANES), "dp", CORE_PAIRS)
    any_space = pl.BlockSpec(memory_space=pl.ANY)
    state = pl.pallas_call(
        state_kernel,
        out_shape=jax.ShapeDtypeStruct((16, 24, LANES), jnp.float32),
        in_specs=[pl.BlockSpec(memory_space=pltpu.SMEM), any_space, any_space, any_space],
        out_specs=VMEM,
        scratch_shapes=[pltpu.VMEM((3, CAP + 2 * EIGHT, LANES), jnp.float32), pltpu.SemaphoreType.DMA((3,))],
        compiler_params=SMALL,
        cost_estimate=pl.CostEstimate(flops=100_000, bytes_accessed=1_000_000, transcendentals=0),
    )(section_rows, old_master, old_first, old_second)
    first_fix, second_fix = corrections(adam_step)
    taken, first_fix, second_fix = lax.optimization_barrier((taken, first_fix, second_fix))
    spread = pl.pallas_call(
        add_kernel,
        out_shape=jax.ShapeDtypeStruct((16, 152, LANES), jnp.float32),
        in_specs=[VMEM, VMEM, VMEM],
        out_specs=VMEM,
        compiler_params=SMALL,
    )(taken, grads, state)
    spread = lax.all_to_all(spread, ("rep", "dp"), 0, 0, axis_index_groups=SPREAD_GROUPS)
    far = pl.pallas_call(
        near_kernel,
        out_shape=jax.ShapeDtypeStruct((16, 40, LANES), jnp.float32),
        in_specs=[VMEM],
        out_specs=VMEM,
        compiler_params=SMALL,
    )(spread)
    far = lax.all_to_all(far, ("rep", "dp"), 0, 0, axis_index_groups=FAR_GROUPS)
    gradient = jnp.sum(far[:, :PIECE], axis=0)
    state = jnp.sum(far[:, PIECE:].reshape(2, 8, 3, EIGHT, LANES), axis=1)
    state = jnp.transpose(state, (1, 0, 2, 3)).reshape(3, PIECE, LANES)
    master, first, second = state
    first = BETA_ONE * first + (1.0 - BETA_ONE) * gradient
    second = BETA_TWO * second + (1.0 - BETA_TWO) * gradient * gradient
    rows = jnp.broadcast_to(jnp.stack((master, first, second)), (8, 3, PIECE, LANES))
    rows = lax.all_to_all(rows, "rep", 0, 0, axis_index_groups=GATHER_GROUPS)
    master, first, second = (rows[:, i].reshape(SHARD, LANES) for i in range(3))
    direction = direction_of(first, second, first_fix, second_fix)
    return (master - RATE * (direction + DECAY * master), first, second, direction)


def solution(mesh):
    in_specs = (
        P("rep", None, None),
        P("rep", None, None),
        P("rep", None, None),
        P("rep", "dp", None, None),
        P(),
        P(),
    )
    out_specs = (P("dp", None), P("dp", None), P("dp", None), P("dp", None))
    return jax.shard_map(local, mesh=mesh, in_specs=in_specs, out_specs=out_specs, check_vma=False)
```

```python
import itertools

import jax
import jax.numpy as jnp
from jax import lax
from jax.experimental import pallas as pl
from jax.experimental.pallas import tpu as pltpu
from jax.sharding import PartitionSpec as P

BETA_ONE = 0.9
BETA_TWO = 0.999
EPSILON = 1e-08
RATE = 0.01
DECAY = 0.1
LANES = 128
CAP = 512
SHARD = 128
PIECE = 16
EIGHT = 8
BITS = (0, 1)
VMEM = pl.BlockSpec(memory_space=pltpu.VMEM)
SMALL = pltpu.CompilerParams(vmem_limit_bytes=8 * 1024 * 1024)


def dp_index(x, z_two, z_one, core):
    return x * 8 + z_two * 4 + z_one * 2 + core


def rep_index(z_hi, y_high, y_one):
    return z_hi * 8 + y_high * 2 + y_one


def flat_index(x, z_two, z_one, core, z_hi, y_high, y_one):
    return rep_index(z_hi, y_high, y_one) * 32 + dp_index(x, z_two, z_one, core)


SPREAD_X, SPREAD_Z, SPREAD_Y = (3, 2, 1, 0), (1, 0), (0, 1)
FAR_TWO, FAR_Z, FAR_Y = (0, 1), (1, 0), (2, 3, 0, 1)
GATHER_LOW, GATHER_HIGH = (0, 1), (2, 3, 0, 1)


def spread_slot(x, z_one, y_one):
    return SPREAD_X.index(x) * 4 + SPREAD_Z.index(z_one) * 2 + SPREAD_Y.index(y_one)


SPREAD_GROUPS = [
    [flat_index(x, z_two, z_one, core, z_hi, y_high, y_one) for x in SPREAD_X for z_one in SPREAD_Z for y_one in SPREAD_Y]
    for z_hi in BITS for y_high in range(4) for z_two in BITS for core in BITS
]
FAR_GROUPS = [
    [flat_index(x, z_two, z_one, core, z_hi, y_high, y_one) for z_two in FAR_TWO for z_hi in FAR_Z for y_high in FAR_Y]
    for y_one in BITS for x in range(4) for z_one in BITS for core in BITS
]
GATHER_GROUPS = [
    [rep_index(z_hi, y_high, y_one) for y_one in GATHER_LOW for y_high in GATHER_HIGH] for z_hi in BITS
]
CORE_PAIRS = [(d, d ^ 1) for d in range(32)]


def corrections(adam_step):
    counted = adam_step[0].astype(jnp.float32)
    first_fix = 1.0 - jnp.power(jnp.float32(BETA_ONE), counted)
    second_fix = 1.0 - jnp.power(jnp.float32(BETA_TWO), counted)
    return first_fix, second_fix


def direction_of(new_first, new_second, first_fix, second_fix):
    return new_first / first_fix / (jnp.sqrt(new_second / second_fix) + EPSILON)


def state_kernel(rows_ref, master_ref, first_ref, second_ref, out_ref, held, sems):
    copies = [
        pltpu.make_async_copy(source.at[0], held.at[i, pl.ds(EIGHT, CAP)], sems.at[i])
        for i, source in enumerate((master_ref, first_ref, second_ref))
    ]
    for copy in copies:
        copy.start()
    rank_rep = lax.axis_index("rep")
    rank_dp = lax.axis_index("dp")
    core = rank_dp % 2
    z_one = (rank_dp // 2) % 2
    z_two = (rank_dp // 4) % 2
    turn = (rank_dp // 8) * 2 + z_one
    begin = jnp.int32(0)
    length = jnp.int32(0)
    for owner in range(16):
        held_rows = rows_ref[owner]
        begin += jnp.where(owner < rank_rep, held_rows, 0)
        length += jnp.where(owner == rank_rep, held_rows, 0)
    piece = sum(jnp.where(turn % 4 == y_high, GATHER_HIGH.index(y_high), 0) for y_high in range(4))
    base = (turn // 4) * (4 * SHARD) + core * SHARD + piece * PIECE + z_two * EIGHT - begin
    place = lax.broadcasted_iota(jnp.int32, (EIGHT, LANES), 0)
    for copy in copies:
        copy.wait()
    for x, other_z, other_y in itertools.product(range(4), BITS, BITS):
        peer = spread_slot(x, other_z, other_y)
        start = base + x * (8 * SHARD) + other_z * (2 * SHARD) + GATHER_LOW.index(other_y) * (SHARD // 2)
        usable = (place >= -start) & (place < length - start)
        at = jnp.clip(start, -EIGHT, CAP) + EIGHT
        for i in range(3):
            rows = held[i, pl.ds(at, EIGHT), :]
            out_ref[peer, i * EIGHT : (i + 1) * EIGHT, :] = jnp.where(usable, rows, 0.0)


def add_kernel(taken_ref, grad_ref, state_ref, out_ref):
    core = lax.axis_index("dp") % 2
    half = SHARD // 2
    for x in range(4):
        for z_two in BITS:
            for z_one in BITS:
                block = x * 4 + z_two * 2 + z_one
                own = pl.multiple_of((block * 2 + core) * SHARD, SHARD)
                total = taken_ref[pl.ds(block * SHARD, SHARD), :] + grad_ref[pl.ds(own, SHARD), :].astype(jnp.float32)
                for y_one in BITS:
                    peer = spread_slot(x, z_one, y_one)
                    first = GATHER_LOW.index(y_one) * half
                    out_ref[peer, z_two * half : (z_two + 1) * half, :] = total[first : first + half]
    out_ref[:, SHARD:, :] = state_ref[...]


def near_kernel(in_ref, out_ref):
    for z_two in BITS:
        for y_high in range(4):
            turn = z_two * 4 + y_high
            rows = pl.ds((z_two * 4 + GATHER_HIGH.index(y_high)) * PIECE, PIECE)
            total = in_ref[0, rows, :]
            for peer in range(1, 16):
                total += in_ref[peer, rows, :]
            source = spread_slot(turn // 2, turn % 2, 0), spread_slot(turn // 2, turn % 2, 1)
            state = in_ref[source[0], SHARD:, :] + in_ref[source[1], SHARD:, :]
            for z_hi in BITS:
                slot = FAR_TWO.index(z_two) * 8 + z_hi * 4 + FAR_Y.index(y_high)
                out_ref[slot, :PIECE, :] = total
                out_ref[slot, PIECE:, :] = state


def local(old_master, old_first, old_second, grad_parts, section_rows, adam_step):
    core = lax.axis_index("dp") % 2
    grads = grad_parts.reshape(32 * SHARD, LANES)
    given = lax.dynamic_index_in_dim(grad_parts.reshape(16, 2, SHARD, LANES), 1 - core, 1, keepdims=False)
    taken = lax.ppermute(given.astype(jnp.float32).reshape(16 * SHARD, LANES), "dp", CORE_PAIRS)
    any_space = pl.BlockSpec(memory_space=pl.ANY)
    state = pl.pallas_call(
        state_kernel,
        out_shape=jax.ShapeDtypeStruct((16, 24, LANES), jnp.float32),
        in_specs=[pl.BlockSpec(memory_space=pltpu.SMEM), any_space, any_space, any_space],
        out_specs=VMEM,
        scratch_shapes=[pltpu.VMEM((3, CAP + 2 * EIGHT, LANES), jnp.float32), pltpu.SemaphoreType.DMA((3,))],
        compiler_params=SMALL,
        cost_estimate=pl.CostEstimate(flops=100_000, bytes_accessed=1_000_000, transcendentals=0),
    )(section_rows, old_master, old_first, old_second)
    first_fix, second_fix = corrections(adam_step)
    taken, first_fix, second_fix = lax.optimization_barrier((taken, first_fix, second_fix))
    spread = pl.pallas_call(
        add_kernel,
        out_shape=jax.ShapeDtypeStruct((16, 152, LANES), jnp.float32),
        in_specs=[VMEM, VMEM, VMEM],
        out_specs=VMEM,
        compiler_params=SMALL,
    )(taken, grads, state)
    spread = lax.all_to_all(spread, ("rep", "dp"), 0, 0, axis_index_groups=SPREAD_GROUPS)
    far = pl.pallas_call(
        near_kernel,
        out_shape=jax.ShapeDtypeStruct((16, 40, LANES), jnp.float32),
        in_specs=[VMEM],
        out_specs=VMEM,
        compiler_params=SMALL,
    )(spread)
    far = lax.all_to_all(far, ("rep", "dp"), 0, 0, axis_index_groups=FAR_GROUPS)
    gradient = jnp.sum(far[:, :PIECE], axis=0)
    state = jnp.sum(far[:, PIECE:].reshape(2, 8, 3, EIGHT, LANES), axis=1)
    state = jnp.stack([state[FAR_TWO.index(z_two)] for z_two in BITS], axis=1).reshape(3, PIECE, LANES)
    master, first, second = state
    first = BETA_ONE * first + (1.0 - BETA_ONE) * gradient
    second = BETA_TWO * second + (1.0 - BETA_TWO) * gradient * gradient
    rows = jnp.broadcast_to(jnp.stack((master, first, second)), (8, 3, PIECE, LANES))
    rows = lax.all_to_all(rows, "rep", 0, 0, axis_index_groups=GATHER_GROUPS)
    master, first, second = (rows[:, i].reshape(SHARD, LANES) for i in range(3))
    direction = direction_of(first, second, first_fix, second_fix)
    return (master - RATE * (direction + DECAY * master), first, second, direction)


def solution(mesh):
    in_specs = (
        P("rep", None, None),
        P("rep", None, None),
        P("rep", None, None),
        P("rep", "dp", None, None),
        P(),
        P(),
    )
    out_specs = (P("dp", None), P("dp", None), P("dp", None), P("dp", None))
    return jax.shard_map(local, mesh=mesh, in_specs=in_specs, out_specs=out_specs, check_vma=False)
```

```python
import itertools

import jax
import jax.numpy as jnp
from jax import lax
from jax.experimental import pallas as pl
from jax.experimental.pallas import tpu as pltpu
from jax.sharding import PartitionSpec as P

BETA_ONE = 0.9
BETA_TWO = 0.999
EPSILON = 1e-08
RATE = 0.01
DECAY = 0.1
LANES = 128
CAP = 512
SHARD = 128
PIECE = 16
EIGHT = 8
BITS = (0, 1)
VMEM = pl.BlockSpec(memory_space=pltpu.VMEM)
SMALL = pltpu.CompilerParams(vmem_limit_bytes=8 * 1024 * 1024)


def dp_index(x, z_two, z_one, core):
    return x * 8 + z_two * 4 + z_one * 2 + core


def rep_index(z_hi, y_high, y_one):
    return z_hi * 8 + y_high * 2 + y_one


def flat_index(x, z_two, z_one, core, z_hi, y_high, y_one):
    return rep_index(z_hi, y_high, y_one) * 32 + dp_index(x, z_two, z_one, core)


SPREAD = [(x, z_one, y_one) for x in (3, 2, 1, 0) for z_one in (1, 0) for y_one in BITS]
FAR = [(z_two, z_hi, y_high) for z_two in BITS for z_hi in (1, 0) for y_high in (2, 0, 3, 1)]
GATHER_HIGH = (2, 3, 0, 1)
SPREAD_GROUPS = [
    [flat_index(x, z_two, z_one, core, z_hi, y_high, y_one) for x, z_one, y_one in SPREAD]
    for z_hi in BITS for y_high in range(4) for z_two in BITS for core in BITS
]
FAR_GROUPS = [
    [flat_index(x, z_two, z_one, core, z_hi, y_high, y_one) for z_two, z_hi, y_high in FAR]
    for y_one in BITS for x in range(4) for z_one in BITS for core in BITS
]
GATHER_GROUPS = [
    [rep_index(z_hi, y_high, y_one) for y_one in BITS for y_high in GATHER_HIGH] for z_hi in BITS
]
CORE_PAIRS = [(d, d ^ 1) for d in range(32)]


def corrections(adam_step):
    counted = adam_step[0].astype(jnp.float32)
    first_fix = 1.0 - jnp.power(jnp.float32(BETA_ONE), counted)
    second_fix = 1.0 - jnp.power(jnp.float32(BETA_TWO), counted)
    return first_fix, second_fix


def direction_of(new_first, new_second, first_fix, second_fix):
    return new_first / first_fix / (jnp.sqrt(new_second / second_fix) + EPSILON)


def state_kernel(rows_ref, master_ref, first_ref, second_ref, out_ref, held, sems):
    copies = [
        pltpu.make_async_copy(source.at[0], held.at[i, pl.ds(EIGHT, CAP)], sems.at[i])
        for i, source in enumerate((master_ref, first_ref, second_ref))
    ]
    for copy in copies:
        copy.start()
    rank_rep = lax.axis_index("rep")
    rank_dp = lax.axis_index("dp")
    core = rank_dp % 2
    z_one = (rank_dp // 2) % 2
    z_two = (rank_dp // 4) % 2
    turn = (rank_dp // 8) * 2 + z_one
    begin = jnp.int32(0)
    length = jnp.int32(0)
    for owner in range(16):
        held_rows = rows_ref[owner]
        begin += jnp.where(owner < rank_rep, held_rows, 0)
        length += jnp.where(owner == rank_rep, held_rows, 0)
    piece = sum(jnp.where(turn % 4 == y_high, GATHER_HIGH.index(y_high), 0) for y_high in range(4))
    base = (turn // 4) * (4 * SHARD) + core * SHARD + piece * PIECE + z_two * EIGHT - begin
    place = lax.broadcasted_iota(jnp.int32, (EIGHT, LANES), 0)
    for copy in copies:
        copy.wait()
    for x, other_z, other_y in itertools.product(range(4), BITS, BITS):
        peer = SPREAD.index((x, other_z, other_y))
        start = base + x * (8 * SHARD) + other_z * (2 * SHARD) + other_y * (SHARD // 2)
        usable = (place >= -start) & (place < length - start)
        at = jnp.clip(start, -EIGHT, CAP) + EIGHT
        for i in range(3):
            rows = held[i, pl.ds(at, EIGHT), :]
            out_ref[peer, i * EIGHT : (i + 1) * EIGHT, :] = jnp.where(usable, rows, 0.0)


def add_kernel(taken_ref, grad_ref, state_ref, out_ref):
    core = lax.axis_index("dp") % 2
    half = SHARD // 2
    for x in range(4):
        for z_two in BITS:
            for z_one in BITS:
                block = x * 4 + z_two * 2 + z_one
                own = pl.multiple_of((block * 2 + core) * SHARD, SHARD)
                total = taken_ref[pl.ds(block * SHARD, SHARD), :] + grad_ref[pl.ds(own, SHARD), :].astype(jnp.float32)
                for y_one in BITS:
                    peer = SPREAD.index((x, z_one, y_one))
                    first = y_one * half
                    out_ref[peer, z_two * half : (z_two + 1) * half, :] = total[first : first + half]
    out_ref[:, SHARD:, :] = state_ref[...]


def near_kernel(in_ref, out_ref):
    for z_two in BITS:
        for y_high in range(4):
            turn = z_two * 4 + y_high
            rows = pl.ds((z_two * 4 + GATHER_HIGH.index(y_high)) * PIECE, PIECE)
            total = in_ref[0, rows, :]
            for peer in range(1, 16):
                total += in_ref[peer, rows, :]
            source = SPREAD.index((turn // 2, turn % 2, 0)), SPREAD.index((turn // 2, turn % 2, 1))
            state = in_ref[source[0], SHARD:, :] + in_ref[source[1], SHARD:, :]
            for z_hi in BITS:
                slot = FAR.index((z_two, z_hi, y_high))
                out_ref[slot, :PIECE, :] = total
                out_ref[slot, PIECE:, :] = state


def local(old_master, old_first, old_second, grad_parts, section_rows, adam_step):
    core = lax.axis_index("dp") % 2
    grads = grad_parts.reshape(32 * SHARD, LANES)
    given = lax.dynamic_index_in_dim(grad_parts.reshape(16, 2, SHARD, LANES), 1 - core, 1, keepdims=False)
    taken = lax.ppermute(given.astype(jnp.float32).reshape(16 * SHARD, LANES), "dp", CORE_PAIRS)
    any_space = pl.BlockSpec(memory_space=pl.ANY)
    state = pl.pallas_call(
        state_kernel,
        out_shape=jax.ShapeDtypeStruct((16, 24, LANES), jnp.float32),
        in_specs=[pl.BlockSpec(memory_space=pltpu.SMEM), any_space, any_space, any_space],
        out_specs=VMEM,
        scratch_shapes=[pltpu.VMEM((3, CAP + 2 * EIGHT, LANES), jnp.float32), pltpu.SemaphoreType.DMA((3,))],
        compiler_params=SMALL,
        cost_estimate=pl.CostEstimate(flops=100_000, bytes_accessed=1_000_000, transcendentals=0),
    )(section_rows, old_master, old_first, old_second)
    first_fix, second_fix = corrections(adam_step)
    taken, first_fix, second_fix = lax.optimization_barrier((taken, first_fix, second_fix))
    spread = pl.pallas_call(
        add_kernel,
        out_shape=jax.ShapeDtypeStruct((16, 152, LANES), jnp.float32),
        in_specs=[VMEM, VMEM, VMEM],
        out_specs=VMEM,
        compiler_params=SMALL,
    )(taken, grads, state)
    spread = lax.all_to_all(spread, ("rep", "dp"), 0, 0, axis_index_groups=SPREAD_GROUPS)
    far = pl.pallas_call(
        near_kernel,
        out_shape=jax.ShapeDtypeStruct((16, 40, LANES), jnp.float32),
        in_specs=[VMEM],
        out_specs=VMEM,
        compiler_params=SMALL,
    )(spread)
    far = lax.all_to_all(far, ("rep", "dp"), 0, 0, axis_index_groups=FAR_GROUPS)
    gradient = jnp.sum(far[:, :PIECE], axis=0)
    rows = far[:, PIECE:].reshape(16, 3, EIGHT, LANES)
    halves = [sum(rows[i] for i in range(16) if FAR[i][0] == z_two) for z_two in BITS]
    state = jnp.stack(halves, axis=1).reshape(3, PIECE, LANES)
    master, first, second = state
    first = BETA_ONE * first + (1.0 - BETA_ONE) * gradient
    second = BETA_TWO * second + (1.0 - BETA_TWO) * gradient * gradient
    rows = jnp.broadcast_to(jnp.stack((master, first, second)), (8, 3, PIECE, LANES))
    rows = lax.all_to_all(rows, "rep", 0, 0, axis_index_groups=GATHER_GROUPS)
    master, first, second = (rows[:, i].reshape(SHARD, LANES) for i in range(3))
    direction = direction_of(first, second, first_fix, second_fix)
    return (master - RATE * (direction + DECAY * master), first, second, direction)


def solution(mesh):
    in_specs = (
        P("rep", None, None),
        P("rep", None, None),
        P("rep", None, None),
        P("rep", "dp", None, None),
        P(),
        P(),
    )
    out_specs = (P("dp", None), P("dp", None), P("dp", None), P("dp", None))
    return jax.shard_map(local, mesh=mesh, in_specs=in_specs, out_specs=out_specs, check_vma=False)
```

```python
import itertools

import jax
import jax.numpy as jnp
from jax import lax
from jax.experimental import pallas as pl
from jax.experimental.pallas import tpu as pltpu
from jax.sharding import PartitionSpec as P

BETA_ONE = 0.9
BETA_TWO = 0.999
EPSILON = 1e-08
RATE = 0.01
DECAY = 0.1
LANES = 128
CAP = 512
SHARD = 128
PIECE = 16
EIGHT = 8
BITS = (0, 1)
VMEM = pl.BlockSpec(memory_space=pltpu.VMEM)
SMALL = pltpu.CompilerParams(vmem_limit_bytes=8 * 1024 * 1024)


def dp_index(x, z_two, z_one, core):
    return x * 8 + z_two * 4 + z_one * 2 + core


def rep_index(z_hi, y_high, y_one):
    return z_hi * 8 + y_high * 2 + y_one


def flat_index(x, z_two, z_one, core, z_hi, y_high, y_one):
    return rep_index(z_hi, y_high, y_one) * 32 + dp_index(x, z_two, z_one, core)


SPREAD = [(x, z_one, y_one) for x in (3, 2, 1, 0) for z_one in (1, 0) for y_one in BITS]
FAR = [(z_two, z_hi, y_high) for z_two in BITS for z_hi in (1, 0) for y_high in (2, 0, 3, 1)]
GATHER_HIGH = (2, 0, 3, 1)
SPREAD_GROUPS = [
    [flat_index(x, z_two, z_one, core, z_hi, y_high, y_one) for x, z_one, y_one in SPREAD]
    for z_hi in BITS for y_high in range(4) for z_two in BITS for core in BITS
]
FAR_GROUPS = [
    [flat_index(x, z_two, z_one, core, z_hi, y_high, y_one) for z_two, z_hi, y_high in FAR]
    for y_one in BITS for x in range(4) for z_one in BITS for core in BITS
]
GATHER_GROUPS = [
    [rep_index(z_hi, y_high, y_one) for y_high in GATHER_HIGH for y_one in BITS] for z_hi in BITS
]
CORE_PAIRS = [(d, d ^ 1) for d in range(32)]


def corrections(adam_step):
    counted = adam_step[0].astype(jnp.float32)
    first_fix = 1.0 - jnp.power(jnp.float32(BETA_ONE), counted)
    second_fix = 1.0 - jnp.power(jnp.float32(BETA_TWO), counted)
    return first_fix, second_fix


def direction_of(new_first, new_second, first_fix, second_fix):
    return new_first / first_fix / (jnp.sqrt(new_second / second_fix) + EPSILON)


def state_kernel(rows_ref, master_ref, first_ref, second_ref, out_ref, held, sems):
    copies = [
        pltpu.make_async_copy(source.at[0], held.at[i, pl.ds(EIGHT, CAP)], sems.at[i])
        for i, source in enumerate((master_ref, first_ref, second_ref))
    ]
    for copy in copies:
        copy.start()
    rank_rep = lax.axis_index("rep")
    rank_dp = lax.axis_index("dp")
    core = rank_dp % 2
    z_one = (rank_dp // 2) % 2
    z_two = (rank_dp // 4) % 2
    turn = (rank_dp // 8) * 2 + z_one
    begin = jnp.int32(0)
    length = jnp.int32(0)
    for owner in range(16):
        held_rows = rows_ref[owner]
        begin += jnp.where(owner < rank_rep, held_rows, 0)
        length += jnp.where(owner == rank_rep, held_rows, 0)
    piece = sum(jnp.where(turn % 4 == y_high, GATHER_HIGH.index(y_high), 0) for y_high in range(4))
    base = (turn // 4) * (4 * SHARD) + core * SHARD + piece * (2 * PIECE) + z_two * EIGHT - begin
    place = lax.broadcasted_iota(jnp.int32, (EIGHT, LANES), 0)
    for copy in copies:
        copy.wait()
    for x, other_z, other_y in itertools.product(range(4), BITS, BITS):
        peer = SPREAD.index((x, other_z, other_y))
        start = base + x * (8 * SHARD) + other_z * (2 * SHARD) + other_y * PIECE
        usable = (place >= -start) & (place < length - start)
        at = jnp.clip(start, -EIGHT, CAP) + EIGHT
        for i in range(3):
            rows = held[i, pl.ds(at, EIGHT), :]
            out_ref[peer, i * EIGHT : (i + 1) * EIGHT, :] = jnp.where(usable, rows, 0.0)


def add_kernel(taken_ref, grad_ref, state_ref, out_ref):
    core = lax.axis_index("dp") % 2
    half = SHARD // 2
    for x in range(4):
        for z_two in BITS:
            for z_one in BITS:
                block = x * 4 + z_two * 2 + z_one
                own = pl.multiple_of((block * 2 + core) * SHARD, SHARD)
                total = taken_ref[pl.ds(block * SHARD, SHARD), :] + grad_ref[pl.ds(own, SHARD), :].astype(jnp.float32)
                for y_one in BITS:
                    peer = SPREAD.index((x, z_one, y_one))
                    for turn in range(4):
                        first, to = (2 * turn + y_one) * PIECE, z_two * half + turn * PIECE
                        out_ref[peer, to : to + PIECE, :] = total[first : first + PIECE]
    out_ref[:, SHARD:, :] = state_ref[...]


def near_kernel(in_ref, out_ref):
    for z_two in BITS:
        for y_high in range(4):
            turn = z_two * 4 + y_high
            rows = pl.ds((z_two * 4 + GATHER_HIGH.index(y_high)) * PIECE, PIECE)
            total = in_ref[0, rows, :]
            for peer in range(1, 16):
                total += in_ref[peer, rows, :]
            source = SPREAD.index((turn // 2, turn % 2, 0)), SPREAD.index((turn // 2, turn % 2, 1))
            state = in_ref[source[0], SHARD:, :] + in_ref[source[1], SHARD:, :]
            for z_hi in BITS:
                slot = FAR.index((z_two, z_hi, y_high))
                out_ref[slot, :PIECE, :] = total
                out_ref[slot, PIECE:, :] = state


def local(old_master, old_first, old_second, grad_parts, section_rows, adam_step):
    core = lax.axis_index("dp") % 2
    grads = grad_parts.reshape(32 * SHARD, LANES)
    given = lax.dynamic_index_in_dim(grad_parts.reshape(16, 2, SHARD, LANES), 1 - core, 1, keepdims=False)
    taken = lax.ppermute(given.astype(jnp.float32).reshape(16 * SHARD, LANES), "dp", CORE_PAIRS)
    any_space = pl.BlockSpec(memory_space=pl.ANY)
    state = pl.pallas_call(
        state_kernel,
        out_shape=jax.ShapeDtypeStruct((16, 24, LANES), jnp.float32),
        in_specs=[pl.BlockSpec(memory_space=pltpu.SMEM), any_space, any_space, any_space],
        out_specs=VMEM,
        scratch_shapes=[pltpu.VMEM((3, CAP + 2 * EIGHT, LANES), jnp.float32), pltpu.SemaphoreType.DMA((3,))],
        compiler_params=SMALL,
        cost_estimate=pl.CostEstimate(flops=100_000, bytes_accessed=1_000_000, transcendentals=0),
    )(section_rows, old_master, old_first, old_second)
    first_fix, second_fix = corrections(adam_step)
    taken, first_fix, second_fix = lax.optimization_barrier((taken, first_fix, second_fix))
    spread = pl.pallas_call(
        add_kernel,
        out_shape=jax.ShapeDtypeStruct((16, 152, LANES), jnp.float32),
        in_specs=[VMEM, VMEM, VMEM],
        out_specs=VMEM,
        compiler_params=SMALL,
    )(taken, grads, state)
    spread = lax.all_to_all(spread, ("rep", "dp"), 0, 0, axis_index_groups=SPREAD_GROUPS)
    far = pl.pallas_call(
        near_kernel,
        out_shape=jax.ShapeDtypeStruct((16, 40, LANES), jnp.float32),
        in_specs=[VMEM],
        out_specs=VMEM,
        compiler_params=SMALL,
    )(spread)
    far = lax.all_to_all(far, ("rep", "dp"), 0, 0, axis_index_groups=FAR_GROUPS)
    gradient = jnp.sum(far[:, :PIECE], axis=0)
    rows = far[:, PIECE:].reshape(16, 3, EIGHT, LANES)
    halves = [sum(rows[i] for i in range(16) if FAR[i][0] == z_two) for z_two in BITS]
    state = jnp.stack(halves, axis=1).reshape(3, PIECE, LANES)
    master, first, second = state
    first = BETA_ONE * first + (1.0 - BETA_ONE) * gradient
    second = BETA_TWO * second + (1.0 - BETA_TWO) * gradient * gradient
    rows = jnp.broadcast_to(jnp.stack((master, first, second)), (8, 3, PIECE, LANES))
    rows = lax.all_to_all(rows, "rep", 0, 0, axis_index_groups=GATHER_GROUPS)
    master, first, second = (rows[:, i].reshape(SHARD, LANES) for i in range(3))
    direction = direction_of(first, second, first_fix, second_fix)
    return (master - RATE * (direction + DECAY * master), first, second, direction)


def solution(mesh):
    in_specs = (
        P("rep", None, None),
        P("rep", None, None),
        P("rep", None, None),
        P("rep", "dp", None, None),
        P(),
        P(),
    )
    out_specs = (P("dp", None), P("dp", None), P("dp", None), P("dp", None))
    return jax.shard_map(local, mesh=mesh, in_specs=in_specs, out_specs=out_specs, check_vma=False)
```

```python
import itertools

import jax
import jax.numpy as jnp
from jax import lax
from jax.experimental import pallas as pl
from jax.experimental.pallas import tpu as pltpu
from jax.sharding import PartitionSpec as P

BETA_ONE = 0.9
BETA_TWO = 0.999
EPSILON = 1e-08
RATE = 0.01
DECAY = 0.1
LANES = 128
CAP = 512
SHARD = 128
PIECE = 16
EIGHT = 8
BITS = (0, 1)
VMEM = pl.BlockSpec(memory_space=pltpu.VMEM)
SMALL = pltpu.CompilerParams(vmem_limit_bytes=8 * 1024 * 1024)


def dp_index(x, z_two, z_one, core):
    return x * 8 + z_two * 4 + z_one * 2 + core


def rep_index(z_hi, y_high, y_one):
    return z_hi * 8 + y_high * 2 + y_one


def flat_index(x, z_two, z_one, core, z_hi, y_high, y_one):
    return rep_index(z_hi, y_high, y_one) * 32 + dp_index(x, z_two, z_one, core)


SPREAD = [(x, z_one, y_one) for x in (3, 2, 1, 0) for z_one in (1, 0) for y_one in BITS]
FAR = [(z_two, z_hi, y_high) for z_two in BITS for y_high in (2, 0, 3, 1) for z_hi in (1, 0)]
GATHER_HIGH = (2, 0, 3, 1)
SPREAD_GROUPS = [
    [flat_index(x, z_two, z_one, core, z_hi, y_high, y_one) for x, z_one, y_one in SPREAD]
    for z_hi in BITS for y_high in range(4) for z_two in BITS for core in BITS
]
FAR_GROUPS = [
    [flat_index(x, z_two, z_one, core, z_hi, y_high, y_one) for z_two, z_hi, y_high in FAR]
    for y_one in BITS for x in range(4) for z_one in BITS for core in BITS
]
GATHER_GROUPS = [
    [rep_index(z_hi, y_high, y_one) for y_high in GATHER_HIGH for y_one in BITS] for z_hi in BITS
]
CORE_PAIRS = [(d, d ^ 1) for d in range(32)]


def corrections(adam_step):
    counted = adam_step[0].astype(jnp.float32)
    first_fix = 1.0 - jnp.power(jnp.float32(BETA_ONE), counted)
    second_fix = 1.0 - jnp.power(jnp.float32(BETA_TWO), counted)
    return first_fix, second_fix


def direction_of(new_first, new_second, first_fix, second_fix):
    return new_first / first_fix / (jnp.sqrt(new_second / second_fix) + EPSILON)


def state_kernel(rows_ref, master_ref, first_ref, second_ref, out_ref, held, sems):
    copies = [
        pltpu.make_async_copy(source.at[0], held.at[i, pl.ds(EIGHT, CAP)], sems.at[i])
        for i, source in enumerate((master_ref, first_ref, second_ref))
    ]
    for copy in copies:
        copy.start()
    rank_rep = lax.axis_index("rep")
    rank_dp = lax.axis_index("dp")
    core = rank_dp % 2
    z_one = (rank_dp // 2) % 2
    z_two = (rank_dp // 4) % 2
    turn = (rank_dp // 8) * 2 + z_one
    begin = jnp.int32(0)
    length = jnp.int32(0)
    for owner in range(16):
        held_rows = rows_ref[owner]
        begin += jnp.where(owner < rank_rep, held_rows, 0)
        length += jnp.where(owner == rank_rep, held_rows, 0)
    piece = sum(jnp.where(turn % 4 == y_high, GATHER_HIGH.index(y_high), 0) for y_high in range(4))
    base = (turn // 4) * (4 * SHARD) + core * SHARD + piece * (2 * PIECE) + z_two * EIGHT - begin
    place = lax.broadcasted_iota(jnp.int32, (EIGHT, LANES), 0)
    for copy in copies:
        copy.wait()
    for x, other_z, other_y in itertools.product(range(4), BITS, BITS):
        peer = SPREAD.index((x, other_z, other_y))
        start = base + x * (8 * SHARD) + other_z * (2 * SHARD) + other_y * PIECE
        usable = (place >= -start) & (place < length - start)
        at = jnp.clip(start, -EIGHT, CAP) + EIGHT
        for i in range(3):
            rows = held[i, pl.ds(at, EIGHT), :]
            out_ref[peer, i * EIGHT : (i + 1) * EIGHT, :] = jnp.where(usable, rows, 0.0)


def add_kernel(taken_ref, grad_ref, state_ref, out_ref):
    core = lax.axis_index("dp") % 2
    half = SHARD // 2
    for x in range(4):
        for z_two in BITS:
            for z_one in BITS:
                block = x * 4 + z_two * 2 + z_one
                own = pl.multiple_of((block * 2 + core) * SHARD, SHARD)
                total = taken_ref[pl.ds(block * SHARD, SHARD), :] + grad_ref[pl.ds(own, SHARD), :].astype(jnp.float32)
                for y_one in BITS:
                    peer = SPREAD.index((x, z_one, y_one))
                    for turn in range(4):
                        first, to = (2 * turn + y_one) * PIECE, z_two * half + turn * PIECE
                        out_ref[peer, to : to + PIECE, :] = total[first : first + PIECE]
    out_ref[:, SHARD:, :] = state_ref[...]


def near_kernel(in_ref, out_ref):
    for z_two in BITS:
        for y_high in range(4):
            turn = z_two * 4 + y_high
            rows = pl.ds((z_two * 4 + GATHER_HIGH.index(y_high)) * PIECE, PIECE)
            total = in_ref[0, rows, :]
            for peer in range(1, 16):
                total += in_ref[peer, rows, :]
            source = SPREAD.index((turn // 2, turn % 2, 0)), SPREAD.index((turn // 2, turn % 2, 1))
            state = in_ref[source[0], SHARD:, :] + in_ref[source[1], SHARD:, :]
            for z_hi in BITS:
                slot = FAR.index((z_two, z_hi, y_high))
                out_ref[slot, :PIECE, :] = total
                out_ref[slot, PIECE:, :] = state


def local(old_master, old_first, old_second, grad_parts, section_rows, adam_step):
    core = lax.axis_index("dp") % 2
    grads = grad_parts.reshape(32 * SHARD, LANES)
    given = lax.dynamic_index_in_dim(grad_parts.reshape(16, 2, SHARD, LANES), 1 - core, 1, keepdims=False)
    taken = lax.ppermute(given.astype(jnp.float32).reshape(16 * SHARD, LANES), "dp", CORE_PAIRS)
    any_space = pl.BlockSpec(memory_space=pl.ANY)
    state = pl.pallas_call(
        state_kernel,
        out_shape=jax.ShapeDtypeStruct((16, 24, LANES), jnp.float32),
        in_specs=[pl.BlockSpec(memory_space=pltpu.SMEM), any_space, any_space, any_space],
        out_specs=VMEM,
        scratch_shapes=[pltpu.VMEM((3, CAP + 2 * EIGHT, LANES), jnp.float32), pltpu.SemaphoreType.DMA((3,))],
        compiler_params=SMALL,
        cost_estimate=pl.CostEstimate(flops=100_000, bytes_accessed=1_000_000, transcendentals=0),
    )(section_rows, old_master, old_first, old_second)
    first_fix, second_fix = corrections(adam_step)
    taken, first_fix, second_fix = lax.optimization_barrier((taken, first_fix, second_fix))
    spread = pl.pallas_call(
        add_kernel,
        out_shape=jax.ShapeDtypeStruct((16, 152, LANES), jnp.float32),
        in_specs=[VMEM, VMEM, VMEM],
        out_specs=VMEM,
        compiler_params=SMALL,
    )(taken, grads, state)
    spread = lax.all_to_all(spread, ("rep", "dp"), 0, 0, axis_index_groups=SPREAD_GROUPS)
    far = pl.pallas_call(
        near_kernel,
        out_shape=jax.ShapeDtypeStruct((16, 40, LANES), jnp.float32),
        in_specs=[VMEM],
        out_specs=VMEM,
        compiler_params=SMALL,
    )(spread)
    far = lax.all_to_all(far, ("rep", "dp"), 0, 0, axis_index_groups=FAR_GROUPS)
    gradient = jnp.sum(far[:, :PIECE], axis=0)
    rows = far[:, PIECE:].reshape(16, 3, EIGHT, LANES)
    halves = [sum(rows[i] for i in range(16) if FAR[i][0] == z_two) for z_two in BITS]
    state = jnp.stack(halves, axis=1).reshape(3, PIECE, LANES)
    master, first, second = state
    first = BETA_ONE * first + (1.0 - BETA_ONE) * gradient
    second = BETA_TWO * second + (1.0 - BETA_TWO) * gradient * gradient
    rows = jnp.broadcast_to(jnp.stack((master, first, second)), (8, 3, PIECE, LANES))
    rows = lax.all_to_all(rows, "rep", 0, 0, axis_index_groups=GATHER_GROUPS)
    master, first, second = (rows[:, i].reshape(SHARD, LANES) for i in range(3))
    direction = direction_of(first, second, first_fix, second_fix)
    return (master - RATE * (direction + DECAY * master), first, second, direction)


def solution(mesh):
    in_specs = (
        P("rep", None, None),
        P("rep", None, None),
        P("rep", None, None),
        P("rep", "dp", None, None),
        P(),
        P(),
    )
    out_specs = (P("dp", None), P("dp", None), P("dp", None), P("dp", None))
    return jax.shard_map(local, mesh=mesh, in_specs=in_specs, out_specs=out_specs, check_vma=False)
```
